128 devices in a mesh: dp: 32 (over x, z, core), ep: 4 (over y).
Axes of the slice: x: 4, y: 4, z: 4, core: 2. Of those that a mesh axis runs over, the one named last changes fastest.
Arguments:
- kv_cache: bfloat16 [8192, 36864], P(('dp', 'ep')), may hold values from -6 to 6
- slot_fill: int32 [8192], P(('dp', 'ep')), may hold values from 0 to 64, as said below
- slot_request: int32 [8192], P(('dp', 'ep')), may hold values from 0 to 3
- moved_slot: int32 [2048], P(('dp', 'ep')), may hold values from 0 to 63, as said below
- moved_target: int32 [2048, 1], P(('dp', 'ep')), may hold values from 0 to 31; in each aligned block of 16 rows (0 to 15, 16 to 31, ...) no two rows name the same one
- queries: bfloat16 [2, 512, 73728], P(None, ('dp', 'ep')), may hold values from -48 to 48
- new_kv: bfloat16 [2, 512, 576], P(None, ('dp', 'ep')), may hold values from -8 to 8
- expert_input: bfloat16 [2, 1024, 3584], P(None, ('dp', 'ep')), may hold values from -6 to 6
- expert_ids: int32 [2, 1024, 8], P(None, ('dp', 'ep')), may hold values from 0 to 63, all different within a row; in each aligned block of 8 rows (0 to 7, 8 to 15, ..., all dimensions but the last counted through in order) at most 2 rows name the same one
- gate_weights: float32 [2, 1024, 8], P(None, ('dp', 'ep')), may hold values from 0.1 to 1
- w_gate: bfloat16 [64, 3584, 1024], P('dp', None, 'ep'), may hold values from -0.09375 to 0.09375
- w_up: bfloat16 [64, 3584, 1024], P('dp', None, 'ep'), may hold values from -0.09375 to 0.09375
- down_weight: bfloat16 [64, 1024, 3584], P('dp', 'ep'), may hold values from -0.1875 to 0.1875
Outputs:
- guest_pages: bfloat16 [4096, 36864], P(('dp', 'ep'))
- attention_out: bfloat16 [2, 512, 65536], P(None, ('dp', 'ep'))
- expert_out: bfloat16 [2, 1024, 3584], P(None, ('dp', 'ep'))
The draws below stay inside these ranges and needn't reach their ends.
Inputs may be any that keep to these rules, and one draw needn't show every extreme that they name: `slot_fill`: valid tokens from the start of the slot; 0 marks a free slot. `slot_request`: the request's index among the 4 requests of the slot's own device. `moved_slot`: the 16 entries of one device name distinct slots of that device. `moved_target`: no dp index is named by more than 1 of the 16 entries of one device. `expert_ids`: the 8 ids of a token are distinct, and in a step no expert is named by more than 2 of the 8 tokens of one device.
All inputs are finite; a program needn't handle non-finite values.
Results may differ from the reference program's by a relative error of at most 0.0065.
Values may be sent and summed in bfloat16 or wider, within the bound.
No kernel may reach another device: no remote copies, remote signals or barrier semaphores. Data moves between devices by JAX's collectives and lax.ppermute only.
A program may use at most 192 MiB of HBM per device.

```python
import math
import jax
import jax.numpy as jnp
import numpy as np
from jax import lax

D = 3584
FF = 1024
H = 128
LAT = 512
PAGE = 64
TOP = 8
STEPS = 2
REQ_DEV = 4
SLOTS_DEV = 64
TOK_DEV = 8
MIG_DEV = 16
MCAP = 1
KVW = 576
FF_DEV = 256
EXPERTS = 64
CAP = 2
REQUESTS = 512
TOKENS = 1024
SLOTS = 8192
MIGS = 2048
GUESTS = 4096
N_DP = 32
N_EP = 4


def shared_latents(key):
    base = jax.random.normal(jax.random.fold_in(key, 11), (STEPS, REQUESTS, KVW), jnp.float32)
    return jnp.clip(base, -5.0, 5.0)


def draw_new_kv(key, part):
    base = shared_latents(key)
    return base.astype(jnp.bfloat16)


def draw_queries(key, part):
    key = jax.random.fold_in(key, 5)
    first_key = jax.random.fold_in(key, 0)
    noise = jnp.clip(jax.random.normal(first_key, (STEPS, REQUESTS, H, KVW), jnp.float32), -6.0, 6.0)
    values = noise
    return values.reshape(STEPS, REQUESTS, H * KVW).astype(jnp.bfloat16)


def draw_slot_fill(key, part):
    key = jax.random.fold_in(key, 7)
    first_key, second_key, third_key = jax.random.split(key, 3)
    device_count = SLOTS // SLOTS_DEV
    used = jax.random.randint(first_key, (device_count, 1), SLOTS_DEV // 4, SLOTS_DEV)
    column = jnp.arange(SLOTS_DEV, dtype=jnp.int32)[None, :]
    partial_fill = jax.random.randint(second_key, (device_count, SLOTS_DEV), 1, PAGE + 1)
    keep_full = (jax.random.randint(third_key, (device_count, SLOTS_DEV), 0, 3) > 0) | (column == 0)
    filled = jnp.where(column < used, jnp.where(keep_full, PAGE, partial_fill), 0)
    return filled.reshape(SLOTS).astype(jnp.int32)


def draw_moved_slot(key, part):
    key = jax.random.fold_in(key, 9)
    device_count = MIGS // MIG_DEV
    scores = jax.random.randint(key, (device_count, SLOTS_DEV), 0, 1 << 20) * SLOTS_DEV
    scores = scores + jnp.arange(SLOTS_DEV, dtype=jnp.int32)[None, :]
    ordered = jnp.argsort(scores, axis=1, stable=True)
    return ordered[:, :MIG_DEV].reshape(MIGS).astype(jnp.int32)


def place_ends(array, stream_key, low, largest):
    longest = array.shape.index(max(array.shape))
    spots = []
    for shift in (0, 1):
        where = [jax.random.randint(jax.random.fold_in(stream_key, axis), (), 0, length) for axis, length in enumerate(array.shape)]
        where[longest] = (where[longest] + shift) % array.shape[longest]
        spots.append(tuple(where))
    return array.at[spots[0]].set(low).at[spots[1]].set(largest)


def block_levels(stream_key, extent, cuts, least, high):
    factor_of = 1.0
    for dim, blocks in cuts:
        steps = jax.random.uniform(jax.random.fold_in(jax.random.fold_in(stream_key, 6), dim), (blocks,), jnp.float32, least / len(cuts), high / len(cuts))
        factor_of = factor_of * jnp.repeat(jnp.exp(steps), extent[dim] // blocks).reshape((-1,) + (1,) * (len(extent) - 1 - dim))
    return factor_of


def shared_out(own_key, own, number, rows, count, top, bound, skew):
    ranking = jax.random.permutation(own_key, count)
    heavy_load, common = load_shares(count, rows * top, bound, skew, True), load_shares(count, rows * top, bound, skew, False)
    places = jnp.arange(count)

    def named(sizes, rotation):
        used = int((sizes > 0).sum())
        fixed = max(1, used // 4)
        passed = fixed + (places - fixed + rotation * (used - fixed)) % max(1, count - fixed)
        return jnp.zeros((count,), jnp.int32).at[ranking[jnp.where(places < fixed, places, passed)]].set(jnp.asarray(sizes, jnp.int32))

    sizes = jnp.where(number % 4 == 0, named(heavy_load, number // 4), named(common, number - number // 4 - 1))
    mixed = jax.random.permutation(jax.random.fold_in(own, 3), count)
    source_of, receiver = mixed[0:count // 2 * 2:2], mixed[1:count // 2 * 2:2]
    room = jnp.minimum(sizes[source_of] - 1, bound - sizes[receiver]) // 2
    room = jnp.where((source_of == ranking[0]) | (receiver == ranking[0]) | (sizes[receiver] == 0), 0, jnp.maximum(room, 0))
    passed = jax.random.randint(jax.random.fold_in(own, 4), (count // 2,), 0, 1 << 20) % (room + 1)
    sizes = sizes.at[source_of].add(-passed).at[receiver].add(passed)
    members = jnp.searchsorted(jnp.cumsum(sizes), jnp.arange(rows * top), side="right").astype(jnp.int32)
    grid = members.reshape(top, rows).T
    grid = grid[jax.random.permutation(jax.random.fold_in(own, 1), rows)]
    rotation = jax.random.randint(jax.random.fold_in(own, 2), (rows, 1), 0, top)
    return jnp.take_along_axis(grid, (jnp.arange(top)[None, :] + rotation) % top, axis=1)


def load_shares(count, total, limit, lean, full):
    loads = [(1 << 20) // math.isqrt(rank ** lean) + 1 for rank in range(1, count + 1)]
    largest = limit if full else min(limit, max(-(-total // count), total * loads[0] // sum(loads)))
    least = 1 if total - largest >= count - 1 else 0
    counts, rest = [largest] + [least] * (count - 1), total - largest - least * (count - 1)
    while rest > 0:
        movable = [i for i in range(1, count) if counts[i] < largest] or [i for i in range(1, count) if counts[i] < limit]
        whole, budget = sum([loads[i] for i in movable]), rest
        for i in movable:
            extra = min(limit - counts[i], max(1, budget * loads[i] // whole), rest)
            counts[i] = counts[i] + extra
            rest = rest - extra
    return np.array(counts)


def scatter_about(stream_key, extent, deviation, limit, shards=(), kind=jnp.bfloat16):
    values = deviation * jax.random.normal(stream_key, extent, jnp.float32)
    if shards:
        values = values * block_levels(stream_key, extent, shards, -0.22, 0.18)
    return jnp.clip(values, -limit, limit).astype(kind)


def setup_inputs(seed: int = 0) -> dict:
    streams_of = jax.random.split(jax.random.key(seed), 14)
    kv_cache = scatter_about(streams_of[0], (SLOTS, PAGE * KVW), 1.0, 6.0, ((0, 128),))
    slot_fill = draw_slot_fill(jax.random.fold_in(streams_of[13], 71), 0)
    slot_request = place_ends(jax.random.randint(streams_of[2], (SLOTS,), 0, REQ_DEV), jax.random.fold_in(streams_of[2], 1), 0, REQ_DEV - 1).astype(jnp.int32)
    moved_slot = draw_moved_slot(jax.random.fold_in(streams_of[13], 71), 0)
    moved_target_keys = jax.random.split(jax.random.fold_in(streams_of[4], 1), MIGS // MIG_DEV)
    moved_target_turns = jax.random.permutation(jax.random.fold_in(streams_of[4], 3), MIGS // MIG_DEV)
    moved_target = jax.vmap(lambda own, number: shared_out(jax.random.fold_in(streams_of[4], 2), own, number, MIG_DEV, N_DP, 1, MCAP, 2))(moved_target_keys, moved_target_turns).reshape((MIGS, 1))
    queries = draw_queries(jax.random.fold_in(streams_of[13], 71), 0)
    new_kv = draw_new_kv(jax.random.fold_in(streams_of[13], 71), 0)
    expert_input = scatter_about(streams_of[7], (STEPS, TOKENS, D), 1.0, 6.0, ((1, 128),))
    expert_ids_keys = jax.random.split(jax.random.fold_in(streams_of[8], 1), STEPS * TOKENS // TOK_DEV)
    expert_ids_turns = jax.random.permutation(jax.random.fold_in(streams_of[8], 3), STEPS * TOKENS // TOK_DEV)
    expert_ids = jax.vmap(lambda own, number: shared_out(jax.random.fold_in(streams_of[8], 2), own, number, TOK_DEV, EXPERTS, TOP, CAP, 2))(expert_ids_keys, expert_ids_turns).reshape((STEPS, TOKENS, TOP))
    gate_weights = jnp.clip(jnp.exp(math.log(1.0) - 2.3025851 * jax.random.uniform(streams_of[9], (STEPS, TOKENS, TOP), jnp.float32) ** block_levels(streams_of[9], (STEPS, TOKENS, TOP), ((1, 128),), -0.2, 0.2)), 0.1, 1.0)
    w_gate = scatter_about(streams_of[10], (EXPERTS, D, FF), D ** -0.5, 0.09375, ((0, 32), (2, 4)))
    w_up = scatter_about(streams_of[11], (EXPERTS, D, FF), D ** -0.5, 0.09375, ((0, 32), (2, 4)))
    down_weight = scatter_about(streams_of[12], (EXPERTS, FF, D), FF ** -0.5, 0.1875, ((0, 32), (1, 4)))
    return dict(kv_cache=kv_cache, slot_fill=slot_fill, slot_request=slot_request, moved_slot=moved_slot, moved_target=moved_target, queries=queries, new_kv=new_kv, expert_input=expert_input, expert_ids=expert_ids, gate_weights=gate_weights, w_gate=w_gate, w_up=w_up, down_weight=down_weight)


MASKED = -1.0e30
SCORE_SCALE = 192.0 ** -0.5
HIGHEST = lax.Precision.HIGHEST


def attend_device(operands):
    query_block, cache_block, fill_block, owner_block, fresh_block = operands
    requests_here = query_block.shape[0]
    query_f = query_block.astype(jnp.float32)
    cache_f = cache_block.astype(jnp.float32)
    fresh_f = fresh_block.astype(jnp.float32)
    slot_query = query_f[owner_block]
    scores = jnp.einsum("shc,spc->shp", slot_query, cache_f, precision=HIGHEST) * SCORE_SCALE
    valid = jnp.arange(cache_block.shape[1], dtype=jnp.int32)[None, :] < fill_block[:, None]
    scores = jnp.where(valid[:, None, :], scores, MASKED)
    slot_top = jnp.max(scores, axis=2)
    member = owner_block[None, :] == jnp.arange(requests_here, dtype=jnp.int32)[:, None]
    cache_top = jnp.max(jnp.where(member[:, :, None], slot_top[None], MASKED), axis=1)
    fresh_scores = jnp.einsum("rhc,jrc->rhj", query_f, fresh_f, precision=HIGHEST) * SCORE_SCALE
    top_score = jnp.maximum(cache_top, jnp.max(fresh_scores, axis=2))
    weights = jnp.where(valid[:, None, :], jnp.exp(scores - top_score[owner_block][:, :, None]), 0.0)
    rounded = weights.astype(jnp.bfloat16).astype(jnp.float32)
    slot_out = jnp.einsum("shp,spc->shc", rounded, cache_f[:, :, :LAT], precision=HIGHEST)
    member_f = member.astype(jnp.float32)
    totals = jnp.dot(member_f, jnp.sum(weights, axis=2), precision=HIGHEST)
    merged = jnp.einsum("rs,shc->rhc", member_f, slot_out, precision=HIGHEST)
    fresh_weights = jnp.exp(fresh_scores - top_score[:, :, None])
    fresh_rounded = fresh_weights.astype(jnp.bfloat16).astype(jnp.float32)
    merged = merged + jnp.einsum("rhj,jrc->rhc", fresh_rounded, fresh_f[:, :, :LAT], precision=HIGHEST)
    totals = totals + jnp.sum(fresh_weights, axis=2)
    return (merged / totals[:, :, None]).astype(jnp.bfloat16).reshape(requests_here, -1)


def run_expert_layer(operands):
    rows_in, gate_mat, up_mat, down_mat = operands
    gate_val = jnp.dot(rows_in, gate_mat, preferred_element_type=jnp.float32)
    up_projection_value = jnp.dot(rows_in, up_mat, preferred_element_type=jnp.float32)
    inner = (jax.nn.silu(gate_val) * up_projection_value).astype(jnp.bfloat16)
    summed = jnp.zeros((rows_in.shape[0], D), jnp.float32)
    for part_index in range(N_EP):
        start = part_index * FF_DEV
        piece = jnp.dot(inner[:, start:start + FF_DEV], down_mat[start:start + FF_DEV], preferred_element_type=jnp.float32)
        summed = summed + piece.astype(jnp.bfloat16).astype(jnp.float32)
    return summed.astype(jnp.bfloat16)


def earlier_same(labels):
    count = labels.shape[1]
    matches = labels[:, :, None] == labels[:, None, :]
    earlier = jnp.arange(count)[None, :] < jnp.arange(count)[:, None]
    return jnp.sum(jnp.where(matches & earlier[None], 1, 0), axis=2).astype(jnp.int32)


def reference(kv_cache, slot_fill, slot_request, moved_slot, moved_target, queries, new_kv, expert_input, expert_ids, gate_weights, w_gate, w_up, down_weight):
    device_count = N_DP * N_EP
    targets = moved_target[:, 0].reshape(device_count, MIG_DEV)
    position = earlier_same(targets)
    source = jnp.arange(device_count, dtype=jnp.int32)[:, None]
    rows_out = ((targets * N_EP + source % N_EP) * N_DP + source // N_EP) * MCAP + position
    rows_in = source * SLOTS_DEV + moved_slot.reshape(device_count, MIG_DEV)
    guest_pages = jnp.zeros((GUESTS, PAGE * KVW), jnp.bfloat16).at[rows_out.reshape(-1)].set(kv_cache[rows_in.reshape(-1)])

    query_all = queries.reshape(STEPS, device_count, REQ_DEV, H, KVW)
    fresh_all = new_kv.reshape(STEPS, device_count, REQ_DEV, KVW)
    cache_all = kv_cache.reshape(device_count, SLOTS_DEV, PAGE, KVW)
    fill_all = slot_fill.reshape(device_count, SLOTS_DEV)
    owner_all = slot_request.reshape(device_count, SLOTS_DEV)
    attention_list = []
    expert_list = []
    for turn_index in range(STEPS):
        fresh_here = jnp.moveaxis(fresh_all[:turn_index + 1], 1, 0)
        result = lax.map(attend_device, (query_all[turn_index], cache_all, fill_all, owner_all, fresh_here))
        attention_list.append(result.reshape(REQUESTS, H * LAT))

        chosen = expert_ids[turn_index].reshape(device_count, TOK_DEV * TOP)
        slot_index = chosen * CAP + earlier_same(chosen)
        resident_tokens = expert_input[turn_index].reshape(device_count, TOK_DEV, D)
        token_of = jnp.arange(TOK_DEV * TOP, dtype=jnp.int32) // TOP
        buffer = jnp.zeros((device_count, EXPERTS * CAP, D), jnp.bfloat16)
        buffer = buffer.at[source, slot_index].set(resident_tokens[:, token_of])
        grouped = buffer.reshape(device_count, EXPERTS, CAP, D).transpose(1, 0, 2, 3).reshape(EXPERTS, device_count * CAP, D)
        produced = lax.map(run_expert_layer, (grouped, w_gate, w_up, down_weight))
        returned = produced.reshape(EXPERTS, device_count, CAP, D).transpose(1, 0, 2, 3).reshape(device_count, EXPERTS * CAP, D)
        selected_experts = jnp.take_along_axis(returned, slot_index[:, :, None], axis=1).astype(jnp.float32)
        selected_experts = selected_experts.reshape(device_count, TOK_DEV, TOP, D)
        scales = gate_weights[turn_index].reshape(device_count, TOK_DEV, TOP)
        mixed = jnp.sum(selected_experts * scales[:, :, :, None], axis=2)
        expert_list.append(mixed.astype(jnp.bfloat16).reshape(TOKENS, D))
    return guest_pages, jnp.stack(attention_list), jnp.stack(expert_list)
```

```python
import jax
import jax.numpy as jnp
from jax import lax
from jax.experimental import pallas as pl
from jax.experimental.pallas import tpu as pltpu
from jax.sharding import PartitionSpec as P

D = 3584
H = 128
LAT = 512
PAGE = 64
TOP = 8
STEPS = 2
REQ = 4
SLOTS = 64
TOK = 8
KVW = 576
FFD = 256
EXPERTS = 64
CAP = 2
DQ = D // 4
XW = D + 128
KPAD = 640
ROWS = STEPS * REQ * H
MASKED = -1e30
SCORE_SCALE = 192.0 ** (-0.5)
VMEM = 56 * 1024 * 1024


def params(**more):
    return pltpu.CompilerParams(vmem_limit_bytes=VMEM, **more)


def iota(shape, dim):
    return lax.broadcasted_iota(jnp.int32, shape, dim)


GRP = 256
SEL = 128


def inner_kernel(base_ref, x_ref, wg_ref, wu_ref, o_ref, xs_ref):
    step = pl.program_id(0)
    base = base_ref[0]
    c_lane = iota((128, SEL), 1)
    pick = (iota((128, SEL), 0) == base + c_lane // 64).astype(jnp.bfloat16)
    code = jnp.dot(x_ref[:, D:], pick, preferred_element_type=jnp.float32)
    row = iota((GRP, SEL), 0)
    col = iota((GRP, SEL), 1)
    here = (row // 8) == (col % 64) // 2
    wanted = (col % 2 + 1).astype(jnp.float32)
    chosen = jnp.where(here & (code == wanted), 1.0, 0.0).astype(jnp.bfloat16)
    sel = lax.dot_general(
        chosen, x_ref[:, :D], (((0,), (0,)), ((), ())), preferred_element_type=jnp.float32
    ).astype(jnp.bfloat16)
    at = lax.rem(step, 4) * 64
    at = pl.multiple_of(at, 64)
    xs_ref[0, pl.ds(at, 64), :] = sel[:64]
    xs_ref[1, pl.ds(at, 64), :] = sel[64:]

    @pl.when(lax.rem(step, 4) == 3)
    def _():
        for e in range(2):
            rows_in = xs_ref[e]
            gate = jnp.dot(rows_in, wg_ref[e], preferred_element_type=jnp.float32)
            up = jnp.dot(rows_in, wu_ref[e], preferred_element_type=jnp.float32)
            o_ref[e] = (gate / (1.0 + jnp.exp(-gate)) * up).astype(jnp.bfloat16)


def inner_of(base, gathered, w_gate, w_up):
    groups = gathered.shape[0] // GRP
    return pl.pallas_call(
        inner_kernel,
        grid=(groups,),
        in_specs=[
            pl.BlockSpec(memory_space=pltpu.SMEM),
            pl.BlockSpec((GRP, XW), lambda i: (i, 0)),
            pl.BlockSpec((2, D, FFD), lambda i: (0, 0, 0)),
            pl.BlockSpec((2, D, FFD), lambda i: (0, 0, 0)),
        ],
        out_specs=pl.BlockSpec((2, 256, FFD), lambda i: (0, i // 4, 0)),
        out_shape=jax.ShapeDtypeStruct((2, groups * 64, FFD), jnp.bfloat16),
        scratch_shapes=[pltpu.VMEM((2, 256, D), jnp.bfloat16)],
        compiler_params=params(dimension_semantics=("arbitrary",)),
        cost_estimate=pl.CostEstimate(
            flops=6_000_000_000, bytes_accessed=24_000_000, transcendentals=300_000
        ),
    )(base, gathered, w_gate, w_up)


def down_kernel(*refs):
    inner, weights, o_ref = refs[:4], refs[4:8], refs[8]
    parts = []
    for e in range(2):
        total = jnp.dot(inner[0][e], weights[0][e], preferred_element_type=jnp.float32)
        for k in range(1, 4):
            total = total + jnp.dot(inner[k][e], weights[k][e], preferred_element_type=jnp.float32)
        parts.append(total.reshape(-1, 8, DQ))
    first, second = parts
    low = iota(first.shape, 1) < 4
    even = jnp.where(low, first, pltpu.roll(second, 4, 1))
    odd = jnp.where(low, pltpu.roll(first, 4, 1), second)
    both = jnp.stack([even, odd], axis=1).reshape(-1, 8, DQ)
    o_ref[...] = both.astype(jnp.bfloat16)


def down_of(inner, weights):
    rows = inner[0].shape[1]
    block = 128
    return pl.pallas_call(
        down_kernel,
        grid=(rows // block,),
        in_specs=[pl.BlockSpec((2, block, FFD), lambda i: (0, i, 0))] * 4
        + [pl.BlockSpec((2, FFD, DQ), lambda i: (0, 0, 0))] * 4,
        out_specs=pl.BlockSpec((block // 4, 8, DQ), lambda i: (i, 0, 0)),
        out_shape=jax.ShapeDtypeStruct((rows // 4, 8, DQ), jnp.bfloat16),
        compiler_params=params(dimension_semantics=("arbitrary",)),
        cost_estimate=pl.CostEstimate(
            flops=2_000_000_000, bytes_accessed=8_000_000, transcendentals=0
        ),
    )(*inner, *weights)


def combine_kernel(mix_ref, ret_ref, o_ref):
    mix = mix_ref[...]
    high = mix.astype(jnp.bfloat16)
    rest = mix - high.astype(jnp.float32)
    mid = rest.astype(jnp.bfloat16)
    low = (rest - mid.astype(jnp.float32)).astype(jnp.bfloat16)
    tokens = mix.shape[0]
    for q in range(4):
        rows = ret_ref[:, q].astype(jnp.float32).reshape(-1, DQ).astype(jnp.bfloat16)
        total = jnp.dot(high, rows, preferred_element_type=jnp.float32)
        total = total + jnp.dot(mid, rows, preferred_element_type=jnp.float32)
        total = total + jnp.dot(low, rows, preferred_element_type=jnp.float32)
        total = total.astype(jnp.bfloat16)
        for s in range(STEPS):
            o_ref[s, :, q * DQ : (q + 1) * DQ] = total[s * TOK : (s + 1) * TOK]


def combine(mix, returned):
    return pl.pallas_call(
        combine_kernel,
        in_specs=[pl.BlockSpec(memory_space=pltpu.VMEM)] * 2,
        out_specs=pl.BlockSpec(memory_space=pltpu.VMEM),
        out_shape=jax.ShapeDtypeStruct((STEPS, TOK, D), jnp.bfloat16),
        compiler_params=params(),
    )(mix, returned.reshape(-1, 4, 8, DQ))


def experts(expert_input, expert_ids, gate_weights, w_gate, w_up, down_weight):
    group = lax.axis_index("dp")
    rank = lax.axis_index("ep")
    ranks = lax.axis_size("ep")

    hits = expert_ids[..., None] == jnp.arange(EXPERTS, dtype=jnp.int32)
    member = jnp.any(hits, axis=2)
    gates = jnp.sum(jnp.where(hits, gate_weights[..., None], 0.0), axis=2)
    counted = member.astype(jnp.int32)
    place = jnp.cumsum(counted, axis=1) - counted
    code = jnp.where(member, place + 1, 0).astype(jnp.bfloat16).reshape(STEPS * TOK, EXPERTS)
    code = jnp.pad(code, ((0, 0), (0, XW - D - EXPERTS)))
    sent = jnp.concatenate([expert_input.reshape(STEPS * TOK, D), code], axis=1)
    gathered = lax.all_gather(sent, ("dp", "ep"), axis=0, tiled=True)

    same = jnp.arange(STEPS)[:, None] == jnp.arange(STEPS)[None, :]
    at_place = place[..., None] == jnp.arange(CAP, dtype=jnp.int32)
    mix = (
        gates[:, :, :, None, None]
        * same[:, None, None, :, None].astype(jnp.float32)
        * at_place[:, :, :, None, :].astype(jnp.float32)
    ).reshape(STEPS * TOK, EXPERTS * STEPS * CAP)

    def shift(array, k):
        return lax.ppermute(array, "ep", [(i, (i + k) % ranks) for i in range(ranks)])

    def columns(k):
        start = lax.rem(rank + k, ranks) * DQ
        return lax.dynamic_slice_in_dim(down_weight, start, DQ, axis=2)

    order = (0, 1, 3, 2)
    weights = [columns(0)] + [shift(columns(k), k) for k in order[1:]]
    base = (2 * group).astype(jnp.int32).reshape(1)
    own = inner_of(base, gathered, w_gate, w_up)
    inner = [own] + [shift(own, k) for k in order[1:]]
    produced = down_of(inner, weights)
    returned = lax.all_to_all(produced, ("dp", "ep"), split_axis=0, concat_axis=0, tiled=True)
    return combine(mix, returned)


def attention_kernel(kv_ref, qe_ref, qo_ref, fresh_ref, fill_ref, owner_ref, o_ref,
                     s_ref, sf_ref, top_ref, total_ref, even_ref, odd_ref):
    nt = (((1,), (1,)), ((), ()))
    pairs = STEPS * REQ
    wide = 4 * SLOTS
    fill = fill_ref[...]
    owner = owner_ref[...]
    inside = iota((1, wide), 1) // SLOTS

    def keys(j, odd):
        pieces = []
        for i in range(4):
            at = pl.multiple_of((4 * j + i) * 1152 + 512 * odd, 128)
            pieces.append(kv_ref[:, pl.ds(at, KPAD)])
        return jnp.concatenate(pieces, axis=0)

    def allowed(j, odd):
        return (8 * j + 2 * inside + odd) < fill

    lane = iota((H, 128), 1)
    for p in range(pairs):
        s, r = p // REQ, p % REQ
        sc = lax.dot_general(qe_ref[p * H : (p + 1) * H], fresh_ref[...], nt,
                             preferred_element_type=jnp.float32) * SCORE_SCALE
        ok = (lane % REQ == r) & (lane // REQ <= s)
        sc = jnp.where(ok, sc, MASKED)
        sf_ref[p * H : (p + 1) * H] = sc
        top_ref[p * H : (p + 1) * H] = jnp.concatenate([sc, sc], axis=1)

    def first(j, carry):
        for odd in range(2):
            k = keys(j, odd)
            ok = allowed(j, odd)
            q_ref = qo_ref if odd else qe_ref
            for p in range(pairs):
                rows = slice(p * H, (p + 1) * H)
                sc = lax.dot_general(q_ref[rows], k, nt, preferred_element_type=jnp.float32)
                sc = jnp.where(ok & (owner == p % REQ), sc * SCORE_SCALE, MASKED)
                s_ref[2 * j + odd, rows] = sc
                top_ref[rows] = jnp.maximum(top_ref[rows], sc)
        return carry

    lax.fori_loop(0, PAGE // 8, first, 0)

    for p in range(pairs):
        rows = slice(p * H, (p + 1) * H)
        top = jnp.max(top_ref[rows], axis=1, keepdims=True)
        top_ref[rows] = jnp.broadcast_to(top, (H, wide))
        w = jnp.exp(sf_ref[rows] - top)
        total_ref[rows] = jnp.concatenate([w, jnp.zeros_like(w)], axis=1)
        even_ref[rows] = jnp.dot(w.astype(jnp.bfloat16), fresh_ref[:, :LAT],
                                 preferred_element_type=jnp.float32)
        odd_ref[rows] = jnp.zeros((H, KPAD), jnp.float32)

    def second(j, carry):
        for odd in range(2):
            k = keys(j, odd)
            for p in range(pairs):
                rows = slice(p * H, (p + 1) * H)
                w = jnp.exp(s_ref[2 * j + odd, rows] - top_ref[rows])
                total_ref[rows] += w
                w = w.astype(jnp.bfloat16)
                if odd:
                    odd_ref[rows] += jnp.dot(w, k, preferred_element_type=jnp.float32)
                else:
                    even_ref[rows] += jnp.dot(w, k[:, :LAT], preferred_element_type=jnp.float32)
        return carry

    lax.fori_loop(0, PAGE // 8, second, 0)

    for p in range(pairs):
        rows = slice(p * H, (p + 1) * H)
        total = jnp.sum(total_ref[rows], axis=1, keepdims=True)
        value = even_ref[rows] + odd_ref[rows, 64 : 64 + LAT]
        o_ref[rows] = (value / total).astype(jnp.bfloat16)


def attention(kv_cache, slot_fill, slot_request, queries, new_kv):
    q = queries.reshape(ROWS, KVW)
    q_even = jnp.pad(q, ((0, 0), (0, KPAD - KVW)))
    q_odd = jnp.pad(q, ((0, 0), (KPAD - KVW, 0)))
    fresh = jnp.pad(new_kv.reshape(STEPS * REQ, KVW), ((0, 128 - STEPS * REQ), (0, KPAD - KVW)))
    fill = jnp.tile(slot_fill, 4).reshape(1, 4 * SLOTS)
    owner = jnp.tile(slot_request, 4).reshape(1, 4 * SLOTS)
    wide = 4 * SLOTS
    out = pl.pallas_call(
        attention_kernel,
        in_specs=[pl.BlockSpec(memory_space=pltpu.VMEM)] * 6,
        out_specs=pl.BlockSpec(memory_space=pltpu.VMEM),
        out_shape=jax.ShapeDtypeStruct((ROWS, LAT), jnp.bfloat16),
        scratch_shapes=[
            pltpu.VMEM((PAGE // 4, ROWS, wide), jnp.float32),
            pltpu.VMEM((ROWS, 128), jnp.float32),
            pltpu.VMEM((ROWS, wide), jnp.float32),
            pltpu.VMEM((ROWS, wide), jnp.float32),
            pltpu.VMEM((ROWS, LAT), jnp.float32),
            pltpu.VMEM((ROWS, KPAD), jnp.float32),
        ],
        compiler_params=params(),
        cost_estimate=pl.CostEstimate(
            flops=20_000_000_000, bytes_accessed=10_000_000, transcendentals=4_000_000
        ),
    )(kv_cache, q_even, q_odd, fresh, fill, owner)
    return out.reshape(STEPS, REQ, H * LAT)


def pages(kv_cache, moved_slot, moved_target):
    groups = lax.axis_size("dp")
    width = kv_cache.shape[1]
    named = jnp.arange(groups, dtype=jnp.int32)[:, None, None] == moved_target[:, 0][None, :, None]
    from_slot = moved_slot[None, :, None] == jnp.arange(SLOTS, dtype=jnp.int32)[None, None, :]
    placing = jnp.any(named & from_slot, axis=1).astype(jnp.bfloat16)
    leaving = jnp.dot(placing, kv_cache, preferred_element_type=jnp.float32).astype(jnp.bfloat16)
    leaving = leaving.reshape(groups, width // 128, 128)
    arrived = lax.all_to_all(leaving, "dp", split_axis=0, concat_axis=0, tiled=True)
    return arrived.reshape(groups, width)


def body(kv_cache, slot_fill, slot_request, moved_slot, moved_target, queries, new_kv,
         expert_input, expert_ids, gate_weights, w_gate, w_up, down_weight):
    expert_out = experts(expert_input, expert_ids, gate_weights, w_gate, w_up, down_weight)
    guest_pages = pages(kv_cache, moved_slot, moved_target)
    attention_out = attention(kv_cache, slot_fill, slot_request, queries, new_kv)
    return guest_pages, attention_out, expert_out


def solution(mesh):
    rows = P(("dp", "ep"), None)
    flat = P(("dp", "ep"))
    second = P(None, ("dp", "ep"), None)
    return jax.shard_map(
        body,
        mesh=mesh,
        in_specs=(rows, flat, flat, flat, rows, second, second, second, second, second,
                  P("dp", None, "ep"), P("dp", None, "ep"), P("dp", "ep", None)),
        out_specs=(rows, second, second),
        check_vma=False,
    )
```

```python
import functools

import jax
import jax.numpy as jnp
from jax import lax
from jax.experimental import pallas as pl
from jax.experimental.pallas import tpu as pltpu
from jax.sharding import PartitionSpec as P

D = 3584
H = 128
LAT = 512
PAGE = 64
TOP = 8
STEPS = 2
REQ = 4
SLOTS = 64
TOK = 8
KVW = 576
FFD = 256
EXPERTS = 64
CAP = 2
DQ = D // 4
XW = D + 128
KPAD = 640
ROWS = STEPS * REQ * H
MASKED = -1e30
SCORE_SCALE = 192.0 ** (-0.5)
ORDER = (0, 1, 3, 2)
VMEM = 56 * 1024 * 1024


def params(**more):
    return pltpu.CompilerParams(vmem_limit_bytes=VMEM, **more)


def iota(shape, dim):
    return lax.broadcasted_iota(jnp.int32, shape, dim)


PIECES_A = tuple((k, other) for k in (0, 1, 3) for other in (0, 1))
PIECES_B = ((2, 0), (2, 1))


def inner_kernel(kinds, parts, place_ref, *refs):
    n = len(kinds)
    pieces, (wg_ref, wu_ref, o_ref, xs_ref) = refs[: n * parts], refs[n * parts :]
    base, px, pz, pc, py = (place_ref[i] for i in range(5))
    row = iota((256, 128), 0)
    col = iota((256, 128), 1)
    pick = (iota((128, 128), 0) == base + iota((128, 128), 1) // 64).astype(jnp.bfloat16)
    same = (row % 16) // 8 == (col % 4) // 2
    same = same & (((py - (row % 64) // 16) & 3) == (col % 16) // 4)
    wanted = (col % 2 + 1).astype(jnp.float32)
    here = []
    for other in range(2):
        at = jnp.where((pc ^ other) == 0, px, pz)
        here.append(same & (((at - row // 64) & 3) == (col % 64) // 16))
    for i, (_, other) in enumerate(kinds):
        x = jnp.concatenate([part[...] for part in pieces[i * parts : (i + 1) * parts]], axis=0)
        code = jnp.dot(x[:, D:], pick, preferred_element_type=jnp.float32)
        chosen = jnp.where(here[other] & (code == wanted), 1.0, 0.0).astype(jnp.bfloat16)
        sel = lax.dot_general(
            chosen, x[:, :D], (((0,), (0,)), ((), ())), preferred_element_type=jnp.float32
        ).astype(jnp.bfloat16)
        xs_ref[0, 64 * i : 64 * i + 64] = sel[:64]
        xs_ref[1, 64 * i : 64 * i + 64] = sel[64:]
    for e in range(2):
        rows_in = xs_ref[e]
        gate = jnp.dot(rows_in, wg_ref[e], preferred_element_type=jnp.float32)
        up = jnp.dot(rows_in, wu_ref[e], preferred_element_type=jnp.float32)
        o_ref[e] = (gate / (1.0 + jnp.exp(-gate)) * up).astype(jnp.bfloat16)


def inner_of(kinds, place, pieces, w_gate, w_up):
    n = len(kinds)
    rows = 64 * n
    return pl.pallas_call(
        functools.partial(inner_kernel, kinds, len(pieces) // n),
        in_specs=[pl.BlockSpec(memory_space=pltpu.SMEM)]
        + [pl.BlockSpec(memory_space=pltpu.VMEM)] * (len(pieces) + 2),
        out_specs=pl.BlockSpec(memory_space=pltpu.VMEM),
        out_shape=jax.ShapeDtypeStruct((2, rows, FFD), jnp.bfloat16),
        scratch_shapes=[pltpu.VMEM((2, rows, D), jnp.bfloat16)],
        compiler_params=params(),
        cost_estimate=pl.CostEstimate(
            flops=1_000_000_000 * n,
            bytes_accessed=7_500_000 + 2_000_000 * n,
            transcendentals=300_000,
        ),
    )(place, *pieces, w_gate, w_up)


def down_kernel(place_ref, *refs):
    inner_a, inner_b, weights = refs[:4], refs[4:8], refs[8:12]
    o_ref, part_ref, held_ref = refs[12:]
    px, pz, pc = (place_ref[i] for i in range(1, 4))
    for inner, at in ((inner_a, 0), (inner_b, 64 * len(PIECES_A))):
        rows = inner[0].shape[1]
        for e in range(2):
            total = None
            for part, weight in zip(inner, weights):
                term = jnp.dot(part[e], weight[e], preferred_element_type=jnp.float32)
                total = term if total is None else total + term
            part_ref[e, at : at + rows] = total.astype(jnp.bfloat16)
    out = iota((256, 128), 0)
    col = iota((256, 128), 1)
    spot = 2 * (col // 64) + col % 2
    for other in range(2):
        step = pc ^ other
        put = (out // 8 == (col % 64) // 2) & (out % 8 == spot + 4 * step)
        put = put.astype(jnp.bfloat16)
        near = jnp.where(step == 0, 32, 8)
        far = 40 - near
        for i, (k, whose) in enumerate(PIECES_A + PIECES_B):
            if whose != other:
                continue
            rows = slice(64 * i, 64 * i + 64)
            part = jnp.concatenate([part_ref[0, rows], part_ref[1, rows]], axis=0)
            placed = jnp.dot(put, part, preferred_element_type=jnp.float32).reshape(32, 8, DQ)
            start = ((jnp.where(step == 0, pz, px) - k) & 3) * far
            for dev in range(32):
                to = start + near * (dev // 8) + 4 * (dev % 2) + (dev % 8) // 2
                if other:
                    o_ref[to] = (held_ref[to] + placed[dev]).astype(jnp.bfloat16)
                else:
                    held_ref[to] = placed[dev]


def down_of(place, inner_a, inner_b, weights):
    rows = inner_a[0].shape[1] + inner_b[0].shape[1]
    return pl.pallas_call(
        down_kernel,
        in_specs=[pl.BlockSpec(memory_space=pltpu.SMEM)] + [pl.BlockSpec(memory_space=pltpu.VMEM)] * 12,
        out_specs=pl.BlockSpec(memory_space=pltpu.VMEM),
        out_shape=jax.ShapeDtypeStruct((128, 8, DQ), jnp.bfloat16),
        scratch_shapes=[
            pltpu.VMEM((2, rows, DQ), jnp.bfloat16),
            pltpu.VMEM((128, 8, DQ), jnp.float32),
        ],
        compiler_params=params(),
        cost_estimate=pl.CostEstimate(
            flops=3_000_000_000, bytes_accessed=8_000_000, transcendentals=0
        ),
    )(place, *inner_a, *inner_b, *weights)


def combine_kernel(mix_ref, ret_ref, o_ref):
    mix = mix_ref[...]
    high = mix.astype(jnp.bfloat16)
    rest = mix - high.astype(jnp.float32)
    mid = rest.astype(jnp.bfloat16)
    low = (rest - mid.astype(jnp.float32)).astype(jnp.bfloat16)
    tokens = mix.shape[0]
    for q in range(4):
        rows = ret_ref[:, q].astype(jnp.float32).reshape(-1, DQ).astype(jnp.bfloat16)
        total = jnp.dot(high, rows, preferred_element_type=jnp.float32)
        total = total + jnp.dot(mid, rows, preferred_element_type=jnp.float32)
        total = total + jnp.dot(low, rows, preferred_element_type=jnp.float32)
        total = total.astype(jnp.bfloat16)
        for s in range(STEPS):
            o_ref[s, :, q * DQ : (q + 1) * DQ] = total[s * TOK : (s + 1) * TOK]


def combine(mix, returned):
    return pl.pallas_call(
        combine_kernel,
        in_specs=[pl.BlockSpec(memory_space=pltpu.VMEM)] * 2,
        out_specs=pl.BlockSpec(memory_space=pltpu.VMEM),
        out_shape=jax.ShapeDtypeStruct((STEPS, TOK, D), jnp.bfloat16),
        compiler_params=params(),
    )(mix, returned.reshape(-1, 4, 8, DQ))


def experts(expert_input, expert_ids, gate_weights, w_gate, w_up, down_weight, prepare, others):
    group = lax.axis_index("dp")
    rank = lax.axis_index("ep")
    ranks = lax.axis_size("ep")
    groups = lax.axis_size("dp")

    hits = expert_ids[..., None] == jnp.arange(EXPERTS, dtype=jnp.int32)
    member = jnp.any(hits, axis=2)
    counted = member.astype(jnp.int32)
    place = jnp.cumsum(counted, axis=1) - counted
    code = jnp.where(member, place + 1, 0).astype(jnp.bfloat16).reshape(STEPS * TOK, EXPERTS)
    code = jnp.pad(code, ((0, 0), (0, XW - D - EXPERTS)))
    sent = jnp.concatenate([expert_input.reshape(STEPS * TOK, D), code], axis=1)

    def over_ep(array, k):
        return lax.ppermute(array, "ep", [(i, (i + k) % ranks) for i in range(ranks)])

    def over_dp(array, move):
        pairs = []
        for i in range(groups):
            x, z, c = move(i // 8, i // 2 % 4, i % 2)
            pairs.append((i, x % 4 * 8 + z % 4 * 2 + c))
        return lax.ppermute(array, "dp", pairs)

    def sibling(array):
        return over_dp(array, lambda x, z, c: (x, z, 1 - c))

    def first_axis(array, k):
        return over_dp(array, lambda x, z, c: (x + k * (1 - c), z + k * c, c))

    def second_axis(array, k):
        return over_dp(array, lambda x, z, c: (x + k * c, z + k * (1 - c), c))

    def spread(array, move):
        return {k: move(array, k) if k else array for k in ORDER}

    def line(parts):
        return jnp.concatenate([parts[k] for k in range(4)], axis=0)

    def columns(k):
        start = lax.rem(rank + k, ranks) * DQ
        return lax.dynamic_slice_in_dim(down_weight, start, DQ, axis=2)

    def mixing(ids, gates):
        hits = ids[..., None] == jnp.arange(EXPERTS, dtype=jnp.int32)
        gates = jnp.sum(jnp.where(hits, gates[..., None], 0.0), axis=2)
        same = jnp.arange(STEPS)[:, None] == jnp.arange(STEPS)[None, :]
        at_place = place[..., None] == jnp.arange(CAP, dtype=jnp.int32)
        return (
            gates.reshape(STEPS, TOK, groups, 1, 2, 1)
            * same[:, None, None, :, None, None].astype(jnp.float32)
            * at_place.reshape(STEPS, TOK, groups, 1, 2, CAP).astype(jnp.float32)
        ).reshape(STEPS * TOK, EXPERTS * STEPS * CAP)

    core = group % 2
    step0, step1 = sent[:TOK], sent[TOK:]
    there = sibling(jnp.where(core == 0, step1, step0))
    chip = jnp.where(
        core == 0,
        jnp.concatenate([step0, there], axis=0),
        jnp.concatenate([there, step1], axis=0),
    )
    column = line(spread(chip, over_ep))
    column, others, expert_ids, gate_weights, down_weight = lax.optimization_barrier(
        (column, others, expert_ids, gate_weights, down_weight)
    )
    where = jnp.stack([2 * group, group // 8, group // 2 % 4, core, rank]).astype(jnp.int32)
    leaving, ready = prepare(others)
    mix = mixing(expert_ids, gate_weights)
    quarters = [columns(k) for k in range(4)]
    plane = line(spread(column, first_axis))
    plane, leaving, mix, where, ready, quarters = lax.optimization_barrier(
        (plane, leaving, mix, where, ready, quarters)
    )
    weights = {0: quarters[0], 1: over_ep(quarters[1], 1), 3: over_ep(quarters[3], 3)}
    pieces = {0: plane, 1: second_axis(plane, 1), 3: second_axis(plane, 3)}
    pieces, weights, opposite = lax.optimization_barrier((pieces, weights, quarters[2]))
    weights[2] = over_ep(opposite, 2)
    early = [p for k in (0, 1, 3) for p in (pieces[k], sibling(pieces[k]))]
    last = [second_axis(pieces[1][:128], 1), second_axis(pieces[3][128:], 3)]

    own_a = inner_of(PIECES_A, where, early, w_gate, w_up)
    inner_a = [over_ep(own_a, k) if k else own_a for k in ORDER]
    last, _, weights, leaving = lax.optimization_barrier((last, own_a, weights, leaving))
    moved = lax.all_to_all(leaving, "dp", split_axis=0, concat_axis=0, tiled=True)
    guests = moved.reshape(groups, -1)
    last = last + [sibling(part) for part in last]
    own_b = inner_of(PIECES_B, where, last, w_gate, w_up)
    inner_b = [over_ep(own_b, k) if k else own_b for k in ORDER]
    produced = down_of(where, inner_a, inner_b, [weights[k] for k in ORDER])
    returned = lax.all_to_all(produced, ("dp", "ep"), split_axis=0, concat_axis=0, tiled=True)
    return combine(mix, returned), guests, ready


def attention_kernel(kv_ref, qe_ref, qo_ref, fresh_ref, fill_ref, owner_ref, o_ref,
                     s_ref, sf_ref, top_ref, total_ref, even_ref, odd_ref, w_ref):
    nt = (((1,), (1,)), ((), ()))
    pairs = STEPS * REQ
    wide = 4 * SLOTS
    fill = fill_ref[...]
    owner = owner_ref[...]
    inside = iota((1, wide), 1) // SLOTS

    def keys(j, odd):
        pieces = []
        for i in range(4):
            at = pl.multiple_of((4 * j + i) * 1152 + 512 * odd, 128)
            pieces.append(kv_ref[:, pl.ds(at, KPAD)])
        return jnp.concatenate(pieces, axis=0)

    def allowed(j, odd):
        return (8 * j + 2 * inside + odd) < fill

    lane = iota((H, 128), 1)
    for p in range(pairs):
        s, r = p // REQ, p % REQ
        sc = lax.dot_general(qe_ref[p * H : (p + 1) * H], fresh_ref[...], nt,
                             preferred_element_type=jnp.float32) * SCORE_SCALE
        ok = (lane % REQ == r) & (lane // REQ <= s)
        sc = jnp.where(ok, sc, MASKED)
        sf_ref[p * H : (p + 1) * H] = sc
        top_ref[p * H : (p + 1) * H] = jnp.concatenate([sc, sc], axis=1)

    def first(j, carry):
        for odd in range(2):
            k = keys(j, odd)
            ok = allowed(j, odd)
            q_ref = qo_ref if odd else qe_ref
            s_ref[2 * j + odd] = lax.dot_general(q_ref[...], k, nt, preferred_element_type=jnp.float32)
            for p in range(pairs):
                rows = slice(p * H, (p + 1) * H)
                sc = s_ref[2 * j + odd, rows] * SCORE_SCALE
                sc = jnp.where(ok & (owner == p % REQ), sc, MASKED)
                s_ref[2 * j + odd, rows] = sc
                top_ref[rows] = jnp.maximum(top_ref[rows], sc)
        return carry

    lax.fori_loop(0, PAGE // 8, first, 0)

    for p in range(pairs):
        rows = slice(p * H, (p + 1) * H)
        top = jnp.max(top_ref[rows], axis=1, keepdims=True)
        top_ref[rows] = jnp.broadcast_to(top, (H, wide))
        w = jnp.exp(sf_ref[rows] - top)
        total_ref[rows] = jnp.concatenate([w, jnp.zeros_like(w)], axis=1)
        even_ref[rows] = jnp.dot(w.astype(jnp.bfloat16), fresh_ref[:, :LAT],
                                 preferred_element_type=jnp.float32)
        odd_ref[rows] = jnp.zeros((H, KPAD), jnp.float32)

    def second(j, carry):
        for odd in range(2):
            k = keys(j, odd)
            for p in range(pairs):
                rows = slice(p * H, (p + 1) * H)
                w = jnp.exp(s_ref[2 * j + odd, rows] - top_ref[rows])
                total_ref[rows] += w
                w_ref[rows] = w.astype(jnp.bfloat16)
            if odd:
                odd_ref[...] += jnp.dot(w_ref[...], k, preferred_element_type=jnp.float32)
            else:
                even_ref[...] += jnp.dot(w_ref[...], k[:, :LAT], preferred_element_type=jnp.float32)
        return carry

    lax.fori_loop(0, PAGE // 8, second, 0)

    for p in range(pairs):
        rows = slice(p * H, (p + 1) * H)
        total = jnp.sum(total_ref[rows], axis=1, keepdims=True)
        value = even_ref[rows] + odd_ref[rows, 64 : 64 + LAT]
        o_ref[rows] = (value / total).astype(jnp.bfloat16)


def attention_operands(slot_fill, slot_request, queries, new_kv):
    q = queries.reshape(ROWS, KVW)
    q_even = jnp.pad(q, ((0, 0), (0, KPAD - KVW)))
    q_odd = jnp.pad(q, ((0, 0), (KPAD - KVW, 0)))
    fresh = jnp.pad(new_kv.reshape(STEPS * REQ, KVW), ((0, 128 - STEPS * REQ), (0, KPAD - KVW)))
    fill = jnp.tile(slot_fill, 4).reshape(1, 4 * SLOTS)
    owner = jnp.tile(slot_request, 4).reshape(1, 4 * SLOTS)
    return q_even, q_odd, fresh, fill, owner


def attention(kv_cache, operands):
    wide = 4 * SLOTS
    out = pl.pallas_call(
        attention_kernel,
        in_specs=[pl.BlockSpec(memory_space=pltpu.VMEM)] * 6,
        out_specs=pl.BlockSpec(memory_space=pltpu.VMEM),
        out_shape=jax.ShapeDtypeStruct((ROWS, LAT), jnp.bfloat16),
        scratch_shapes=[
            pltpu.VMEM((PAGE // 4, ROWS, wide), jnp.float32),
            pltpu.VMEM((ROWS, 128), jnp.float32),
            pltpu.VMEM((ROWS, wide), jnp.float32),
            pltpu.VMEM((ROWS, wide), jnp.float32),
            pltpu.VMEM((ROWS, LAT), jnp.float32),
            pltpu.VMEM((ROWS, KPAD), jnp.float32),
            pltpu.VMEM((ROWS, wide), jnp.bfloat16),
        ],
        compiler_params=params(),
        cost_estimate=pl.CostEstimate(
            flops=20_000_000_000, bytes_accessed=10_000_000, transcendentals=4_000_000
        ),
    )(kv_cache, *operands)
    return out.reshape(STEPS, REQ, H * LAT)


def leaving_pages(kv_cache, moved_slot, moved_target):
    groups = lax.axis_size("dp")
    width = kv_cache.shape[1]
    named = jnp.arange(groups, dtype=jnp.int32)[:, None, None] == moved_target[:, 0][None, :, None]
    from_slot = moved_slot[None, :, None] == jnp.arange(SLOTS, dtype=jnp.int32)[None, None, :]
    placing = jnp.any(named & from_slot, axis=1).astype(jnp.bfloat16)
    leaving = jnp.dot(placing, kv_cache, preferred_element_type=jnp.float32).astype(jnp.bfloat16)
    return leaving.reshape(groups, width // 128, 128)


def body(kv_cache, slot_fill, slot_request, moved_slot, moved_target, queries, new_kv,
         expert_input, expert_ids, gate_weights, w_gate, w_up, down_weight):
    def prepare(others):
        slots, targets, *rest = others
        return leaving_pages(kv_cache, slots, targets), attention_operands(*rest)

    others = (moved_slot, moved_target, slot_fill, slot_request, queries, new_kv)
    expert_out, guest_pages, ready = experts(
        expert_input, expert_ids, gate_weights, w_gate, w_up, down_weight, prepare, others
    )
    attention_out = attention(kv_cache, ready)
    return guest_pages, attention_out, expert_out


def solution(mesh):
    rows = P(("dp", "ep"), None)
    flat = P(("dp", "ep"))
    second = P(None, ("dp", "ep"), None)
    return jax.shard_map(
        body,
        mesh=mesh,
        in_specs=(rows, flat, flat, flat, rows, second, second, second, second, second,
                  P("dp", None, "ep"), P("dp", None, "ep"), P("dp", "ep", None)),
        out_specs=(rows, second, second),
        check_vma=False,
    )
```

```python
import collections
import functools

import jax
import jax.numpy as jnp
from jax import lax
from jax.experimental import pallas as pl
from jax.experimental.pallas import tpu as pltpu
from jax.sharding import PartitionSpec as P

D = 3584
H = 128
LAT = 512
PAGE = 64
TOP = 8
STEPS = 2
REQ = 4
SLOTS = 64
TOK = 8
KVW = 576
FFD = 256
EXPERTS = 64
CAP = 2
DQ = D // 4
XW = D + 128
KPAD = 640
ROWS = STEPS * REQ * H
MASKED = -1e30
SCORE_SCALE = 192.0 ** (-0.5)
ORDER = (0, 1, 3, 2)
VMEM = 56 * 1024 * 1024


def params(**more):
    return pltpu.CompilerParams(vmem_limit_bytes=VMEM, **more)


def iota(shape, dim):
    return lax.broadcasted_iota(jnp.int32, shape, dim)


PIECES_A = tuple((k, other) for k in (0, 1, 3) for other in (0, 1))
PIECES_B = ((2, 0), (2, 1))


def inner_kernel(kinds, parts, place_ref, *refs):
    n = len(kinds)
    pieces, (wg_ref, wu_ref, *before, o_ref, xs_ref) = refs[: n * parts], refs[n * parts :]
    skip = before[0].shape[1] if before else 0
    for earlier in before:
        o_ref[:, :skip] = earlier[...]
    base, px, pz, pc, py = (place_ref[i] for i in range(5))
    row = iota((256, 128), 0)
    col = iota((256, 128), 1)
    pick = (iota((128, 128), 0) == base + iota((128, 128), 1) // 64).astype(jnp.bfloat16)
    same = (row % 16) // 8 == (col % 4) // 2
    same = same & (((py - (row % 64) // 16) & 3) == (col % 16) // 4)
    wanted = (col % 2 + 1).astype(jnp.float32)
    here = []
    for other in range(2):
        at = jnp.where((pc ^ other) == 0, px, pz)
        here.append(same & (((at - row // 64) & 3) == (col % 64) // 16))
    for i, (_, other) in enumerate(kinds):
        x = jnp.concatenate([part[...] for part in pieces[i * parts : (i + 1) * parts]], axis=0)
        code = jnp.dot(x[:, D:], pick, preferred_element_type=jnp.float32)
        chosen = jnp.where(here[other] & (code == wanted), 1.0, 0.0).astype(jnp.bfloat16)
        sel = lax.dot_general(
            chosen, x[:, :D], (((0,), (0,)), ((), ())), preferred_element_type=jnp.float32
        ).astype(jnp.bfloat16)
        xs_ref[0, 64 * i : 64 * i + 64] = sel[:64]
        xs_ref[1, 64 * i : 64 * i + 64] = sel[64:]
    for e in range(2):
        rows_in = xs_ref[e]
        gate = jnp.dot(rows_in, wg_ref[e], preferred_element_type=jnp.float32)
        up = jnp.dot(rows_in, wu_ref[e], preferred_element_type=jnp.float32)
        o_ref[e, skip:] = (gate / (1.0 + jnp.exp(-gate)) * up).astype(jnp.bfloat16)


def inner_of(kinds, place, pieces, w_gate, w_up, *before):
    n = len(kinds)
    rows = 64 * n
    skip = before[0].shape[1] if before else 0
    return pl.pallas_call(
        functools.partial(inner_kernel, kinds, len(pieces) // n),
        in_specs=[pl.BlockSpec(memory_space=pltpu.SMEM)]
        + [pl.BlockSpec(memory_space=pltpu.VMEM)] * (len(pieces) + 2 + len(before)),
        out_specs=pl.BlockSpec(memory_space=pltpu.VMEM),
        out_shape=jax.ShapeDtypeStruct((2, skip + rows, FFD), jnp.bfloat16),
        scratch_shapes=[pltpu.VMEM((2, rows, D), jnp.bfloat16)],
        compiler_params=params(),
        cost_estimate=pl.CostEstimate(
            flops=1_000_000_000 * n,
            bytes_accessed=7_500_000 + 2_000_000 * n,
            transcendentals=300_000,
        ),
    )(place, *pieces, w_gate, w_up, *before)


def down_kernel(place_ref, *refs):
    inner_a, inner_b, weights = refs[:4], refs[4:8], refs[8:13]
    o_ref, part_ref, held_ref = refs[13:]
    px, pz, pc = (place_ref[i] for i in range(1, 4))
    for inner, at in ((inner_a, 0), (inner_b, 64 * len(PIECES_A))):
        rows = inner[0].shape[1]
        for e in range(2):
            total = None
            parts = [weights[i][e] for i in range(3)] + [weights[3 + e][0]]
            for part, weight in zip(inner, parts):
                term = jnp.dot(part[e], weight, preferred_element_type=jnp.float32)
                total = term if total is None else total + term
            part_ref[e, at : at + rows] = total.astype(jnp.bfloat16)
    out = iota((256, 128), 0)
    col = iota((256, 128), 1)
    spot = 2 * (col // 64) + col % 2
    for other in range(2):
        step = pc ^ other
        put = (out // 8 == (col % 64) // 2) & (out % 8 == spot + 4 * step)
        put = put.astype(jnp.bfloat16)
        near = jnp.where(step == 0, 32, 8)
        far = 40 - near
        for i, (k, whose) in enumerate(PIECES_A + PIECES_B):
            if whose != other:
                continue
            rows = slice(64 * i, 64 * i + 64)
            part = jnp.concatenate([part_ref[0, rows], part_ref[1, rows]], axis=0)
            placed = jnp.dot(put, part, preferred_element_type=jnp.float32).reshape(32, 8, DQ)
            start = ((jnp.where(step == 0, pz, px) - k) & 3) * far
            for dev in range(32):
                to = start + near * (dev // 8) + 4 * (dev % 2) + (dev % 8) // 2
                if other:
                    o_ref[to] = (held_ref[to] + placed[dev]).astype(jnp.bfloat16)
                else:
                    held_ref[to] = placed[dev]


def down_of(place, inner_a, inner_b, weights):
    rows = inner_a[0].shape[1] + inner_b[0].shape[1]
    return pl.pallas_call(
        down_kernel,
        in_specs=[pl.BlockSpec(memory_space=pltpu.SMEM)] + [pl.BlockSpec(memory_space=pltpu.VMEM)] * 13,
        out_specs=pl.BlockSpec(memory_space=pltpu.VMEM),
        out_shape=jax.ShapeDtypeStruct((128, 8, DQ), jnp.bfloat16),
        scratch_shapes=[
            pltpu.VMEM((2, rows, DQ), jnp.bfloat16),
            pltpu.VMEM((128, 8, DQ), jnp.float32),
        ],
        compiler_params=params(),
        cost_estimate=pl.CostEstimate(
            flops=3_000_000_000, bytes_accessed=8_000_000, transcendentals=0
        ),
    )(place, *inner_a, *inner_b, *weights)


def combine_kernel(mix_ref, ret_ref, o_ref):
    mix = mix_ref[...]
    high = mix.astype(jnp.bfloat16)
    rest = mix - high.astype(jnp.float32)
    mid = rest.astype(jnp.bfloat16)
    low = (rest - mid.astype(jnp.float32)).astype(jnp.bfloat16)
    tokens = mix.shape[0]
    for q in range(4):
        rows = ret_ref[:, q].astype(jnp.float32).reshape(-1, DQ).astype(jnp.bfloat16)
        total = jnp.dot(high, rows, preferred_element_type=jnp.float32)
        total = total + jnp.dot(mid, rows, preferred_element_type=jnp.float32)
        total = total + jnp.dot(low, rows, preferred_element_type=jnp.float32)
        total = total.astype(jnp.bfloat16)
        for s in range(STEPS):
            o_ref[s, :, q * DQ : (q + 1) * DQ] = total[s * TOK : (s + 1) * TOK]


def combine(mix, returned):
    return pl.pallas_call(
        combine_kernel,
        in_specs=[pl.BlockSpec(memory_space=pltpu.VMEM)] * 2,
        out_specs=pl.BlockSpec(memory_space=pltpu.VMEM),
        out_shape=jax.ShapeDtypeStruct((STEPS, TOK, D), jnp.bfloat16),
        compiler_params=params(),
    )(mix, returned.reshape(-1, 4, 8, DQ))


def experts(expert_input, expert_ids, gate_weights, w_gate, w_up, down_weight, hooks, paged, others):
    group = lax.axis_index("dp")
    rank = lax.axis_index("ep")
    ranks = lax.axis_size("ep")
    groups = lax.axis_size("dp")

    hits = expert_ids[..., None] == jnp.arange(EXPERTS, dtype=jnp.int32)
    member = jnp.any(hits, axis=2)
    counted = member.astype(jnp.int32)
    place = jnp.cumsum(counted, axis=1) - counted
    code = jnp.where(member, place + 1, 0).astype(jnp.bfloat16).reshape(STEPS * TOK, EXPERTS)
    code = jnp.pad(code, ((0, 0), (0, XW - D - EXPERTS)))
    sent = jnp.concatenate([expert_input.reshape(STEPS * TOK, D), code], axis=1)

    def over_ep(array, k):
        return lax.ppermute(array, "ep", [(i, (i + k) % ranks) for i in range(ranks)])

    def over_dp(array, move):
        pairs = []
        for i in range(groups):
            x, z, c = move(i // 8, i // 2 % 4, i % 2)
            pairs.append((i, x % 4 * 8 + z % 4 * 2 + c))
        return lax.ppermute(array, "dp", pairs)

    def sibling(array):
        return over_dp(array, lambda x, z, c: (x, z, 1 - c))

    def first_axis(array, k):
        return over_dp(array, lambda x, z, c: (x + k * (1 - c), z + k * c, c))

    def second_axis(array, k):
        return over_dp(array, lambda x, z, c: (x + k * c, z + k * (1 - c), c))

    def spread(array, move):
        return {k: move(array, k) if k else array for k in ORDER}

    def line(parts):
        return jnp.concatenate([parts[k] for k in range(4)], axis=0)

    def columns(k):
        start = lax.rem(rank + k, ranks) * DQ
        return lax.dynamic_slice_in_dim(down_weight, start, DQ, axis=2)

    def mixing(ids, gates):
        hits = ids[..., None] == jnp.arange(EXPERTS, dtype=jnp.int32)
        gates = jnp.sum(jnp.where(hits, gates[..., None], 0.0), axis=2)
        same = jnp.arange(STEPS)[:, None] == jnp.arange(STEPS)[None, :]
        at_place = place[..., None] == jnp.arange(CAP, dtype=jnp.int32)
        return (
            gates.reshape(STEPS, TOK, groups, 1, 2, 1)
            * same[:, None, None, :, None, None].astype(jnp.float32)
            * at_place.reshape(STEPS, TOK, groups, 1, 2, CAP).astype(jnp.float32)
        ).reshape(STEPS * TOK, EXPERTS * STEPS * CAP)

    core = group % 2
    step0, step1 = sent[:TOK], sent[TOK:]
    there = sibling(jnp.where(core == 0, step1, step0))
    chip = jnp.where(
        core == 0,
        jnp.concatenate([step0, there], axis=0),
        jnp.concatenate([there, step1], axis=0),
    )
    column = line(spread(chip, over_ep))
    quarters = [columns(k) for k in range(4)]
    parts = (quarters[2][:1], quarters[2][1:])
    column, others, expert_ids, gate_weights, quarters, parts = lax.optimization_barrier(
        (column, others, expert_ids, gate_weights, quarters, parts)
    )
    where = jnp.stack([2 * group, group // 8, group // 2 % 4, core, rank]).astype(jnp.int32)
    ready = hooks.operands(*others)
    mix = mixing(expert_ids, gate_weights)
    opposite = [over_ep(parts[0], 2)]
    plane = line(spread(column, first_axis))
    plane, paged, mix, where, ready, quarters, opposite = lax.optimization_barrier(
        (plane, paged, mix, where, ready, quarters, opposite)
    )
    weights = {0: quarters[0], 1: over_ep(quarters[1], 1), 3: over_ep(quarters[3], 3)}
    pieces = {1: second_axis(plane, 1), 3: second_axis(plane, 3)}
    own_a = inner_of(PIECES_A[:2], where, [plane, sibling(plane)], w_gate, w_up)
    leaving = hooks.leaving(*paged)
    pieces, own_a, weights, rest, leaving = lax.optimization_barrier(
        (pieces, own_a, weights, parts[1], leaving)
    )
    opposite.append(over_ep(rest, 2))
    early = [p for k in (1, 3) for p in (pieces[k], sibling(pieces[k]))]
    last = [second_axis(pieces[1][:128], 1), second_axis(pieces[3][128:], 3)]

    own_a = inner_of(PIECES_A[2:], where, early, w_gate, w_up, own_a)
    inner_a = [over_ep(own_a, k) if k else own_a for k in ORDER]
    last, _, opposite, leaving = lax.optimization_barrier((last, own_a, opposite, leaving))
    moved = lax.all_to_all(leaving, "dp", split_axis=0, concat_axis=0, tiled=True)
    guests = moved.reshape(groups, -1)
    last = last + [sibling(part) for part in last]
    own_b = inner_of(PIECES_B, where, last, w_gate, w_up)
    inner_b = [over_ep(own_b, k) if k else own_b for k in ORDER]
    produced = down_of(where, inner_a, inner_b, [weights[k] for k in ORDER[:3]] + opposite)
    returned = lax.all_to_all(produced, ("dp", "ep"), split_axis=0, concat_axis=0, tiled=True)
    return combine(mix, returned), guests, ready


def attention_kernel(kv_ref, qe_ref, qo_ref, fresh_ref, fill_ref, owner_ref, o_ref,
                     s_ref, sf_ref, top_ref, total_ref, even_ref, odd_ref, w_ref):
    nt = (((1,), (1,)), ((), ()))
    pairs = STEPS * REQ
    wide = 4 * SLOTS
    fill = fill_ref[...]
    owner = owner_ref[...]
    inside = iota((1, wide), 1) // SLOTS

    def keys(j, odd):
        pieces = []
        for i in range(4):
            at = pl.multiple_of((4 * j + i) * 1152 + 512 * odd, 128)
            pieces.append(kv_ref[:, pl.ds(at, KPAD)])
        return jnp.concatenate(pieces, axis=0)

    def allowed(j, odd):
        return (8 * j + 2 * inside + odd) < fill

    lane = iota((H, 128), 1)
    for p in range(pairs):
        s, r = p // REQ, p % REQ
        sc = lax.dot_general(qe_ref[p * H : (p + 1) * H], fresh_ref[...], nt,
                             preferred_element_type=jnp.float32)
        ok = (lane % REQ == r) & (lane // REQ <= s)
        sc = jnp.where(ok, sc, MASKED)
        sf_ref[p * H : (p + 1) * H] = sc
        top_ref[p * H : (p + 1) * H] = jnp.concatenate([sc, sc], axis=1)

    def first(j, carry):
        for odd in range(2):
            k = keys(j, odd)
            ok = allowed(j, odd)
            q_ref = qo_ref if odd else qe_ref
            s_ref[2 * j + odd] = lax.dot_general(q_ref[...], k, nt, preferred_element_type=jnp.float32)
            for p in range(pairs):
                rows = slice(p * H, (p + 1) * H)
                sc = jnp.where(ok & (owner == p % REQ), s_ref[2 * j + odd, rows], MASKED)
                top_ref[rows] = jnp.maximum(top_ref[rows], sc)
        return carry

    lax.fori_loop(0, PAGE // 8, first, 0)

    for p in range(pairs):
        rows = slice(p * H, (p + 1) * H)
        top = jnp.max(top_ref[rows], axis=1, keepdims=True) * SCORE_SCALE
        top_ref[rows] = jnp.broadcast_to(top, (H, wide))
        w = jnp.exp(sf_ref[rows] * SCORE_SCALE - top)
        total_ref[rows] = jnp.concatenate([w, jnp.zeros_like(w)], axis=1)
        even_ref[rows] = jnp.dot(w.astype(jnp.bfloat16), fresh_ref[:, :LAT],
                                 preferred_element_type=jnp.float32)
        odd_ref[rows] = jnp.zeros((H, KPAD), jnp.float32)

    def second(jj, carry):
        for odd in range(2):
            for half in range(2):
                j = 2 * jj + half
                ok = allowed(j, odd)
                for p in range(pairs):
                    rows = slice(p * H, (p + 1) * H)
                    w = jnp.exp(s_ref[2 * j + odd, rows] * SCORE_SCALE - top_ref[rows])
                    w = jnp.where(ok & (owner == p % REQ), w, 0.0)
                    total_ref[rows] += w
                    w_ref[rows, half * wide : (half + 1) * wide] = w.astype(jnp.bfloat16)
            k = jnp.concatenate([keys(2 * jj, odd), keys(2 * jj + 1, odd)], axis=0)
            if odd:
                odd_ref[...] += jnp.dot(w_ref[...], k, preferred_element_type=jnp.float32)
            else:
                even_ref[...] += jnp.dot(w_ref[...], k[:, :LAT], preferred_element_type=jnp.float32)
        return carry

    lax.fori_loop(0, PAGE // 16, second, 0)

    for p in range(pairs):
        rows = slice(p * H, (p + 1) * H)
        total = jnp.sum(total_ref[rows], axis=1, keepdims=True)
        value = even_ref[rows] + odd_ref[rows, 64 : 64 + LAT]
        o_ref[rows] = (value / total).astype(jnp.bfloat16)


def attention_operands(slot_fill, slot_request, queries, new_kv):
    q = queries.reshape(ROWS, KVW)
    q_even = jnp.pad(q, ((0, 0), (0, KPAD - KVW)))
    q_odd = jnp.pad(q, ((0, 0), (KPAD - KVW, 0)))
    fresh = jnp.pad(new_kv.reshape(STEPS * REQ, KVW), ((0, 128 - STEPS * REQ), (0, KPAD - KVW)))
    fill = jnp.tile(slot_fill, 4).reshape(1, 4 * SLOTS)
    owner = jnp.tile(slot_request, 4).reshape(1, 4 * SLOTS)
    return q_even, q_odd, fresh, fill, owner


def attention(kv_cache, operands):
    wide = 4 * SLOTS
    out = pl.pallas_call(
        attention_kernel,
        in_specs=[pl.BlockSpec(memory_space=pltpu.VMEM)] * 6,
        out_specs=pl.BlockSpec(memory_space=pltpu.VMEM),
        out_shape=jax.ShapeDtypeStruct((ROWS, LAT), jnp.bfloat16),
        scratch_shapes=[
            pltpu.VMEM((PAGE // 4, ROWS, wide), jnp.float32),
            pltpu.VMEM((ROWS, 128), jnp.float32),
            pltpu.VMEM((ROWS, wide), jnp.float32),
            pltpu.VMEM((ROWS, wide), jnp.float32),
            pltpu.VMEM((ROWS, LAT), jnp.float32),
            pltpu.VMEM((ROWS, KPAD), jnp.float32),
            pltpu.VMEM((ROWS, 2 * wide), jnp.bfloat16),
        ],
        compiler_params=params(),
        cost_estimate=pl.CostEstimate(
            flops=20_000_000_000, bytes_accessed=10_000_000, transcendentals=4_000_000
        ),
    )(kv_cache, *operands)
    return out.reshape(STEPS, REQ, H * LAT)


def leaving_pages(kv_cache, moved_slot, moved_target):
    groups = lax.axis_size("dp")
    width = kv_cache.shape[1]
    named = jnp.arange(groups, dtype=jnp.int32)[:, None, None] == moved_target[:, 0][None, :, None]
    from_slot = moved_slot[None, :, None] == jnp.arange(SLOTS, dtype=jnp.int32)[None, None, :]
    placing = jnp.any(named & from_slot, axis=1).astype(jnp.bfloat16)
    leaving = jnp.dot(placing, kv_cache, preferred_element_type=jnp.float32).astype(jnp.bfloat16)
    return leaving.reshape(groups, width // 128, 128)


Hooks = collections.namedtuple("Hooks", "operands leaving")


def body(kv_cache, slot_fill, slot_request, moved_slot, moved_target, queries, new_kv,
         expert_input, expert_ids, gate_weights, w_gate, w_up, down_weight):
    hooks = Hooks(attention_operands, functools.partial(leaving_pages, kv_cache))
    expert_out, guest_pages, ready = experts(
        expert_input, expert_ids, gate_weights, w_gate, w_up, down_weight, hooks,
        (moved_slot, moved_target), (slot_fill, slot_request, queries, new_kv),
    )
    attention_out = attention(kv_cache, ready)
    return guest_pages, attention_out, expert_out


def solution(mesh):
    rows = P(("dp", "ep"), None)
    flat = P(("dp", "ep"))
    second = P(None, ("dp", "ep"), None)
    return jax.shard_map(
        body,
        mesh=mesh,
        in_specs=(rows, flat, flat, flat, rows, second, second, second, second, second,
                  P("dp", None, "ep"), P("dp", None, "ep"), P("dp", "ep", None)),
        out_specs=(rows, second, second),
        check_vma=False,
    )
```

```python
import collections
import functools

import jax
import jax.numpy as jnp
from jax import lax
from jax.experimental import pallas as pl
from jax.experimental.pallas import tpu as pltpu
from jax.sharding import PartitionSpec as P

D = 3584
H = 128
LAT = 512
PAGE = 64
TOP = 8
STEPS = 2
REQ = 4
SLOTS = 64
TOK = 8
KVW = 576
FFD = 256
EXPERTS = 64
CAP = 2
DQ = D // 4
XW = D + 128
KPAD = 640
ROWS = STEPS * REQ * H
MASKED = -1e30
SCORE_SCALE = 192.0 ** (-0.5)
ORDER = (0, 1, 3, 2)
VMEM = 56 * 1024 * 1024


def params(**more):
    return pltpu.CompilerParams(vmem_limit_bytes=VMEM, **more)


def iota(shape, dim):
    return lax.broadcasted_iota(jnp.int32, shape, dim)


PIECES_A = tuple((k, other) for k in (0, 1, 3) for other in (0, 1))
PIECES_B = ((2, 0), (2, 1))


def inner_kernel(kinds, parts, place_ref, *refs):
    n = len(kinds)
    pieces, (wg_ref, wu_ref, *before, o_ref, xs_ref) = refs[: n * parts], refs[n * parts :]
    skip = before[0].shape[1] if before else 0
    for earlier in before:
        o_ref[:, :skip] = earlier[...]
    base, px, pz, pc, py = (place_ref[i] for i in range(5))
    row = iota((256, 128), 0)
    col = iota((256, 128), 1)
    pick = (iota((128, 128), 0) == base + iota((128, 128), 1) // 64).astype(jnp.bfloat16)
    same = (row % 16) // 8 == (col % 4) // 2
    same = same & (((py - (row % 64) // 16) & 3) == (col % 16) // 4)
    wanted = (col % 2 + 1).astype(jnp.float32)
    here = []
    for other in range(2):
        at = jnp.where((pc ^ other) == 0, px, pz)
        here.append(same & (((at - row // 64) & 3) == (col % 64) // 16))
    for i, (_, other) in enumerate(kinds):
        x = jnp.concatenate([part[...] for part in pieces[i * parts : (i + 1) * parts]], axis=0)
        code = jnp.dot(x[:, D:], pick, preferred_element_type=jnp.float32)
        chosen = jnp.where(here[other] & (code == wanted), 1.0, 0.0).astype(jnp.bfloat16)
        sel = lax.dot_general(
            chosen, x[:, :D], (((0,), (0,)), ((), ())), preferred_element_type=jnp.float32
        ).astype(jnp.bfloat16)
        xs_ref[0, 64 * i : 64 * i + 64] = sel[:64]
        xs_ref[1, 64 * i : 64 * i + 64] = sel[64:]
    for e in range(2):
        rows_in = xs_ref[e]
        gate = jnp.dot(rows_in, wg_ref[e], preferred_element_type=jnp.float32)
        up = jnp.dot(rows_in, wu_ref[e], preferred_element_type=jnp.float32)
        o_ref[e, skip:] = (gate / (1.0 + jnp.exp(-gate)) * up).astype(jnp.bfloat16)


def inner_of(kinds, place, pieces, w_gate, w_up, *before):
    n = len(kinds)
    rows = 64 * n
    skip = before[0].shape[1] if before else 0
    return pl.pallas_call(
        functools.partial(inner_kernel, kinds, len(pieces) // n),
        in_specs=[pl.BlockSpec(memory_space=pltpu.SMEM)]
        + [pl.BlockSpec(memory_space=pltpu.VMEM)] * (len(pieces) + 2 + len(before)),
        out_specs=pl.BlockSpec(memory_space=pltpu.VMEM),
        out_shape=jax.ShapeDtypeStruct((2, skip + rows, FFD), jnp.bfloat16),
        scratch_shapes=[pltpu.VMEM((2, rows, D), jnp.bfloat16)],
        compiler_params=params(),
        cost_estimate=pl.CostEstimate(
            flops=1_000_000_000 * n,
            bytes_accessed=7_500_000 + 2_000_000 * n,
            transcendentals=300_000,
        ),
    )(place, *pieces, w_gate, w_up, *before)


def down_kernel(place_ref, *refs):
    inner_a, inner_b, weights = refs[:4], refs[4:8], refs[8:13]
    o_ref, part_ref, held_ref = refs[13:]
    px, pz, pc = (place_ref[i] for i in range(1, 4))
    for inner, at in ((inner_a, 0), (inner_b, 64 * len(PIECES_A))):
        rows = inner[0].shape[1]
        for e in range(2):
            total = None
            parts = [weights[i][e] for i in range(3)] + [weights[3 + e][0]]
            for part, weight in zip(inner, parts):
                term = jnp.dot(part[e], weight, preferred_element_type=jnp.float32)
                total = term if total is None else total + term
            part_ref[e, at : at + rows] = total.astype(jnp.bfloat16)
    out = iota((256, 128), 0)
    col = iota((256, 128), 1)
    spot = 2 * (col // 64) + col % 2
    for other in range(2):
        step = pc ^ other
        put = (out // 8 == (col % 64) // 2) & (out % 8 == spot + 4 * step)
        put = put.astype(jnp.bfloat16)
        near = jnp.where(step == 0, 32, 8)
        far = 40 - near
        for i, (k, whose) in enumerate(PIECES_A + PIECES_B):
            if whose != other:
                continue
            rows = slice(64 * i, 64 * i + 64)
            part = jnp.concatenate([part_ref[0, rows], part_ref[1, rows]], axis=0)
            placed = jnp.dot(put, part, preferred_element_type=jnp.float32).reshape(32, 8, DQ)
            start = ((jnp.where(step == 0, pz, px) - k) & 3) * far
            for dev in range(32):
                to = start + near * (dev // 8) + 4 * (dev % 2) + (dev % 8) // 2
                if other:
                    o_ref[to] = (held_ref[to] + placed[dev]).astype(jnp.bfloat16)
                else:
                    held_ref[to] = placed[dev]


def down_of(place, inner_a, inner_b, weights):
    rows = inner_a[0].shape[1] + inner_b[0].shape[1]
    return pl.pallas_call(
        down_kernel,
        in_specs=[pl.BlockSpec(memory_space=pltpu.SMEM)] + [pl.BlockSpec(memory_space=pltpu.VMEM)] * 13,
        out_specs=pl.BlockSpec(memory_space=pltpu.VMEM),
        out_shape=jax.ShapeDtypeStruct((128, 8, DQ), jnp.bfloat16),
        scratch_shapes=[
            pltpu.VMEM((2, rows, DQ), jnp.bfloat16),
            pltpu.VMEM((128, 8, DQ), jnp.float32),
        ],
        compiler_params=params(),
        cost_estimate=pl.CostEstimate(
            flops=3_000_000_000, bytes_accessed=8_000_000, transcendentals=0
        ),
    )(place, *inner_a, *inner_b, *weights)


def combine_kernel(mix_ref, ret_ref, o_ref):
    mix = mix_ref[...]
    high = mix.astype(jnp.bfloat16)
    rest = mix - high.astype(jnp.float32)
    mid = rest.astype(jnp.bfloat16)
    low = (rest - mid.astype(jnp.float32)).astype(jnp.bfloat16)
    tokens = mix.shape[0]
    three = jnp.concatenate([high, mid, low], axis=0)
    for q in range(4):
        rows = ret_ref[:, q].astype(jnp.float32).reshape(-1, DQ).astype(jnp.bfloat16)
        total = jnp.dot(three, rows, preferred_element_type=jnp.float32)
        total = total[:tokens] + total[tokens : 2 * tokens] + total[2 * tokens :]
        total = total.astype(jnp.bfloat16)
        for s in range(STEPS):
            o_ref[s, :, q * DQ : (q + 1) * DQ] = total[s * TOK : (s + 1) * TOK]


def combine(mix, returned):
    return pl.pallas_call(
        combine_kernel,
        in_specs=[pl.BlockSpec(memory_space=pltpu.VMEM)] * 2,
        out_specs=pl.BlockSpec(memory_space=pltpu.VMEM),
        out_shape=jax.ShapeDtypeStruct((STEPS, TOK, D), jnp.bfloat16),
        compiler_params=params(),
    )(mix, returned.reshape(-1, 4, 8, DQ))


def experts(expert_input, expert_ids, gate_weights, w_gate, w_up, down_weight, hooks, paged, others):
    group = lax.axis_index("dp")
    rank = lax.axis_index("ep")
    ranks = lax.axis_size("ep")
    groups = lax.axis_size("dp")

    hits = expert_ids[..., None] == jnp.arange(EXPERTS, dtype=jnp.int32)
    member = jnp.any(hits, axis=2)
    counted = member.astype(jnp.int32)
    place = jnp.cumsum(counted, axis=1) - counted
    code = jnp.where(member, place + 1, 0).astype(jnp.bfloat16).reshape(STEPS * TOK, EXPERTS)
    code = jnp.pad(code, ((0, 0), (0, XW - D - EXPERTS)))
    sent = jnp.concatenate([expert_input.reshape(STEPS * TOK, D), code], axis=1)

    def over_ep(array, k):
        return lax.ppermute(array, "ep", [(i, (i + k) % ranks) for i in range(ranks)])

    def over_dp(array, move):
        pairs = []
        for i in range(groups):
            x, z, c = move(i // 8, i // 2 % 4, i % 2)
            pairs.append((i, x % 4 * 8 + z % 4 * 2 + c))
        return lax.ppermute(array, "dp", pairs)

    def sibling(array):
        return over_dp(array, lambda x, z, c: (x, z, 1 - c))

    def first_axis(array, k):
        return over_dp(array, lambda x, z, c: (x + k * (1 - c), z + k * c, c))

    def second_axis(array, k):
        return over_dp(array, lambda x, z, c: (x + k * c, z + k * (1 - c), c))

    def spread(array, move):
        return {k: move(array, k) if k else array for k in ORDER}

    def line(parts):
        return jnp.concatenate([parts[k] for k in range(4)], axis=0)

    def columns(k):
        start = lax.rem(rank + k, ranks) * DQ
        return lax.dynamic_slice_in_dim(down_weight, start, DQ, axis=2)

    def mixing(ids, gates):
        hits = ids[..., None] == jnp.arange(EXPERTS, dtype=jnp.int32)
        gates = jnp.sum(jnp.where(hits, gates[..., None], 0.0), axis=2)
        same = jnp.arange(STEPS)[:, None] == jnp.arange(STEPS)[None, :]
        at_place = place[..., None] == jnp.arange(CAP, dtype=jnp.int32)
        return (
            gates.reshape(STEPS, TOK, groups, 1, 2, 1)
            * same[:, None, None, :, None, None].astype(jnp.float32)
            * at_place.reshape(STEPS, TOK, groups, 1, 2, CAP).astype(jnp.float32)
        ).reshape(STEPS * TOK, EXPERTS * STEPS * CAP)

    core = group % 2
    step0, step1 = sent[:TOK], sent[TOK:]
    there = sibling(jnp.where(core == 0, step1, step0))
    chip = jnp.where(
        core == 0,
        jnp.concatenate([step0, there], axis=0),
        jnp.concatenate([there, step1], axis=0),
    )
    column = line(spread(chip, over_ep))
    quarters = [columns(k) for k in range(4)]
    parts = (quarters[2][:1], quarters[2][1:])
    column, others, expert_ids, gate_weights, quarters, parts = lax.optimization_barrier(
        (column, others, expert_ids, gate_weights, quarters, parts)
    )
    where = jnp.stack([2 * group, group // 8, group // 2 % 4, core, rank]).astype(jnp.int32)
    ready = hooks.operands(*others)
    mix = mixing(expert_ids, gate_weights)
    opposite = [over_ep(parts[0], 2)]
    plane = line(spread(column, first_axis))
    plane, paged, mix, where, ready, quarters, opposite = lax.optimization_barrier(
        (plane, paged, mix, where, ready, quarters, opposite)
    )
    weights = {0: quarters[0], 1: over_ep(quarters[1], 1), 3: over_ep(quarters[3], 3)}
    pieces = {1: second_axis(plane, 1), 3: second_axis(plane, 3)}
    own_a = inner_of(PIECES_A[:2], where, [plane, sibling(plane)], w_gate, w_up)
    leaving = hooks.leaving(*paged)
    pieces, own_a, weights, rest, leaving = lax.optimization_barrier(
        (pieces, own_a, weights, parts[1], leaving)
    )
    opposite.append(over_ep(rest, 2))
    early = [p for k in (1, 3) for p in (pieces[k], sibling(pieces[k]))]
    last = [second_axis(pieces[1][:128], 1), second_axis(pieces[3][128:], 3)]

    own_a = inner_of(PIECES_A[2:], where, early, w_gate, w_up, own_a)
    inner_a = [over_ep(own_a, k) if k else own_a for k in ORDER]
    last, _, opposite, leaving = lax.optimization_barrier((last, own_a, opposite, leaving))
    moved = lax.all_to_all(leaving, "dp", split_axis=0, concat_axis=0, tiled=True)
    guests = moved.reshape(groups, -1)
    last = last + [sibling(part) for part in last]
    own_b = inner_of(PIECES_B, where, last, w_gate, w_up)
    inner_b = [over_ep(own_b, k) if k else own_b for k in ORDER]
    produced = down_of(where, inner_a, inner_b, [weights[k] for k in ORDER[:3]] + opposite)
    returned = lax.all_to_all(produced, ("dp", "ep"), split_axis=0, concat_axis=0, tiled=True)
    return combine(mix, returned), guests, ready


def attention_kernel(kv_ref, qe_ref, qo_ref, fresh_ref, fill_ref, owner_ref, o_ref,
                     s_ref, sf_ref, top_ref, total_ref, even_ref, odd_ref, w_ref):
    nt = (((1,), (1,)), ((), ()))
    pairs = STEPS * REQ
    wide = 4 * SLOTS
    fill = fill_ref[...]
    owner = owner_ref[...]
    inside = iota((1, wide), 1) // SLOTS

    def keys(j, odd):
        pieces = []
        for i in range(4):
            at = pl.multiple_of((4 * j + i) * 1152 + 512 * odd, 128)
            pieces.append(kv_ref[:, pl.ds(at, KPAD)])
        return jnp.concatenate(pieces, axis=0)

    def allowed(j, odd):
        return (8 * j + 2 * inside + odd) < fill

    lane = iota((H, 128), 1)
    for p in range(pairs):
        s, r = p // REQ, p % REQ
        sc = lax.dot_general(qe_ref[p * H : (p + 1) * H], fresh_ref[...], nt,
                             preferred_element_type=jnp.float32)
        ok = (lane % REQ == r) & (lane // REQ <= s)
        sc = jnp.where(ok, sc, MASKED)
        sf_ref[p * H : (p + 1) * H] = sc
        top_ref[p * H : (p + 1) * H] = jnp.concatenate([sc, sc], axis=1)

    def first(j, carry):
        for odd in range(2):
            k = keys(j, odd)
            ok = allowed(j, odd)
            q_ref = qo_ref if odd else qe_ref
            s_ref[2 * j + odd] = lax.dot_general(q_ref[...], k, nt, preferred_element_type=jnp.float32)
            for p in range(pairs):
                rows = slice(p * H, (p + 1) * H)
                sc = jnp.where(ok & (owner == p % REQ), s_ref[2 * j + odd, rows], MASKED)
                top_ref[rows] = jnp.maximum(top_ref[rows], sc)
        return carry

    lax.fori_loop(0, PAGE // 8, first, 0)

    for p in range(pairs):
        rows = slice(p * H, (p + 1) * H)
        top = jnp.max(top_ref[rows], axis=1, keepdims=True) * SCORE_SCALE
        top_ref[rows] = jnp.broadcast_to(top, (H, wide))
        w = jnp.exp(sf_ref[rows] * SCORE_SCALE - top)
        total_ref[rows] = jnp.concatenate([w, jnp.zeros_like(w)], axis=1)
        even_ref[rows] = jnp.dot(w.astype(jnp.bfloat16), fresh_ref[:, :LAT],
                                 preferred_element_type=jnp.float32)
        odd_ref[rows] = jnp.zeros((H, KPAD), jnp.float32)

    def second(jj, carry):
        for odd in range(2):
            for half in range(2):
                j = 2 * jj + half
                ok = allowed(j, odd)
                for p in range(pairs):
                    rows = slice(p * H, (p + 1) * H)
                    w = jnp.exp(s_ref[2 * j + odd, rows] * SCORE_SCALE - top_ref[rows])
                    w = jnp.where(ok & (owner == p % REQ), w, 0.0)
                    total_ref[rows] += w
                    w_ref[rows, half * wide : (half + 1) * wide] = w.astype(jnp.bfloat16)
            k = jnp.concatenate([keys(2 * jj, odd), keys(2 * jj + 1, odd)], axis=0)
            if odd:
                odd_ref[...] += jnp.dot(w_ref[...], k, preferred_element_type=jnp.float32)
            else:
                even_ref[...] += jnp.dot(w_ref[...], k[:, :LAT], preferred_element_type=jnp.float32)
        return carry

    lax.fori_loop(0, PAGE // 16, second, 0)

    for p in range(pairs):
        rows = slice(p * H, (p + 1) * H)
        total = jnp.sum(total_ref[rows], axis=1, keepdims=True)
        value = even_ref[rows] + odd_ref[rows, 64 : 64 + LAT]
        o_ref[rows] = (value / total).astype(jnp.bfloat16)


def attention_operands(slot_fill, slot_request, queries, new_kv):
    q = queries.reshape(ROWS, KVW)
    q_even = jnp.pad(q, ((0, 0), (0, KPAD - KVW)))
    q_odd = jnp.pad(q, ((0, 0), (KPAD - KVW, 0)))
    fresh = jnp.pad(new_kv.reshape(STEPS * REQ, KVW), ((0, 128 - STEPS * REQ), (0, KPAD - KVW)))
    fill = jnp.tile(slot_fill, 4).reshape(1, 4 * SLOTS)
    owner = jnp.tile(slot_request, 4).reshape(1, 4 * SLOTS)
    return q_even, q_odd, fresh, fill, owner


def attention(kv_cache, operands):
    wide = 4 * SLOTS
    out = pl.pallas_call(
        attention_kernel,
        in_specs=[pl.BlockSpec(memory_space=pltpu.VMEM)] * 6,
        out_specs=pl.BlockSpec(memory_space=pltpu.VMEM),
        out_shape=jax.ShapeDtypeStruct((ROWS, LAT), jnp.bfloat16),
        scratch_shapes=[
            pltpu.VMEM((PAGE // 4, ROWS, wide), jnp.float32),
            pltpu.VMEM((ROWS, 128), jnp.float32),
            pltpu.VMEM((ROWS, wide), jnp.float32),
            pltpu.VMEM((ROWS, wide), jnp.float32),
            pltpu.VMEM((ROWS, LAT), jnp.float32),
            pltpu.VMEM((ROWS, KPAD), jnp.float32),
            pltpu.VMEM((ROWS, 2 * wide), jnp.bfloat16),
        ],
        compiler_params=params(),
        cost_estimate=pl.CostEstimate(
            flops=20_000_000_000, bytes_accessed=10_000_000, transcendentals=4_000_000
        ),
    )(kv_cache, *operands)
    return out.reshape(STEPS, REQ, H * LAT)


def leaving_pages(kv_cache, moved_slot, moved_target):
    groups = lax.axis_size("dp")
    width = kv_cache.shape[1]
    named = jnp.arange(groups, dtype=jnp.int32)[:, None, None] == moved_target[:, 0][None, :, None]
    from_slot = moved_slot[None, :, None] == jnp.arange(SLOTS, dtype=jnp.int32)[None, None, :]
    placing = jnp.any(named & from_slot, axis=1).astype(jnp.bfloat16)
    leaving = jnp.dot(placing, kv_cache, preferred_element_type=jnp.float32).astype(jnp.bfloat16)
    return leaving.reshape(groups, width // 128, 128)


Hooks = collections.namedtuple("Hooks", "operands leaving")


def body(kv_cache, slot_fill, slot_request, moved_slot, moved_target, queries, new_kv,
         expert_input, expert_ids, gate_weights, w_gate, w_up, down_weight):
    hooks = Hooks(attention_operands, functools.partial(leaving_pages, kv_cache))
    expert_out, guest_pages, ready = experts(
        expert_input, expert_ids, gate_weights, w_gate, w_up, down_weight, hooks,
        (moved_slot, moved_target), (slot_fill, slot_request, queries, new_kv),
    )
    attention_out = attention(kv_cache, ready)
    return guest_pages, attention_out, expert_out


def solution(mesh):
    rows = P(("dp", "ep"), None)
    flat = P(("dp", "ep"))
    second = P(None, ("dp", "ep"), None)
    return jax.shard_map(
        body,
        mesh=mesh,
        in_specs=(rows, flat, flat, flat, rows, second, second, second, second, second,
                  P("dp", None, "ep"), P("dp", None, "ep"), P("dp", "ep", None)),
        out_specs=(rows, second, second),
        check_vma=False,
    )
```
